32 devices in a mesh: row: 8 (over y, x, core), col: 4 (over z).
Axes of the slice: x: 2, y: 2, z: 4, core: 2. Of those that a mesh axis runs over, the one named last changes fastest.
Arguments:
- activations: bfloat16 [256, 64, 5120], P(('row', 'col')), may hold values from -6 to 6
- out_grads: bfloat16 [256, 64, 8192], P(('row', 'col')), may hold values from -6 to 6
- lengths: int32 [256], P(('row', 'col')), may hold values from 16 to 64
- proj_in: bfloat16 [5120, 128], replicated, may hold values from -0.078125 to 0.078125
- proj_out: bfloat16 [8192, 128], replicated, may hold values from -0.0625 to 0.0625
Outputs:
- fisher: float32 [16384, 16384], P('row', 'col')
The draws below stay inside these ranges and needn't reach their ends.
All inputs are finite; a program needn't handle non-finite values.
Results may differ from the reference program's by a relative error of at most 0.0068.
Values may be sent and summed in bfloat16 or wider, within the bound.
A program may use at most 128 MiB of HBM per device.

```python
import jax
import jax.numpy as jnp

D = 5120
Q = 8192
RANK = 128
L = 64
EXAMPLES = 256
ORDER = 16384


def touch_ends(array, stream_key, low, largest):
    longest = array.shape.index(max(array.shape))
    spots = []
    for shift in (0, 1):
        where = [jax.random.randint(jax.random.fold_in(stream_key, axis), (), 0, length) for axis, length in enumerate(array.shape)]
        where[longest] = (where[longest] + shift) % array.shape[longest]
        spots.append(tuple(where))
    return array.at[spots[0]].set(low).at[spots[1]].set(largest)


def block_levels(rng, extent, shards, least, top_value):
    gain = 1.0
    for dim, shards_of in shards:
        heights = jax.random.uniform(jax.random.fold_in(jax.random.fold_in(rng, 6), dim), (shards_of,), jnp.float32, least / len(shards), top_value / len(shards))
        gain = gain * jnp.repeat(jnp.exp(heights), extent[dim] // shards_of).reshape((-1,) + (1,) * (len(extent) - 1 - dim))
    return gain


def bell_draw(own_key, shape, width, most, pieces=(), kind=jnp.bfloat16):
    values = jax.random.normal(own_key, shape, jnp.float32) * width
    if len(pieces) > 0:
        values = block_levels(own_key, shape, pieces, -0.22, 0.18) * values
    return jnp.clip(values, min=-most, max=most).astype(kind)


def setup_inputs(seed: int = 0) -> dict:
    seeds = jax.random.split(jax.random.key(seed), 6)
    activations = bell_draw(seeds[0], (EXAMPLES, L, D), 1.0, 6.0, ((0, 32),))
    out_grads = bell_draw(seeds[1], (EXAMPLES, L, Q), 1.0, 6.0, ((0, 32),))
    lengths = touch_ends(jax.random.randint(seeds[2], (EXAMPLES,), L // 4, L + 1), jax.random.fold_in(seeds[2], 1), L // 4, L).astype(jnp.int32)
    proj_in = bell_draw(seeds[3], (D, RANK), D ** -0.5, 0.078125)
    proj_out = bell_draw(seeds[4], (Q, RANK), Q ** -0.5, 0.0625)
    return dict(activations=activations, out_grads=out_grads, lengths=lengths, proj_in=proj_in, proj_out=proj_out)


def reference(activations, out_grads, lengths, proj_in, proj_out):
    in_factors = jnp.einsum('etd,dr->etr', activations.astype(jnp.float32), proj_in.astype(jnp.float32)).astype(jnp.bfloat16)
    out_raw = jnp.einsum('etq,qr->etr', out_grads.astype(jnp.float32), proj_out.astype(jnp.float32))
    positions = jnp.arange(L, dtype=jnp.int32)
    valid = (positions[None, :] < lengths[:, None]).astype(jnp.float32)
    out_factors = (out_raw * valid[:, :, None]).astype(jnp.bfloat16)
    grads = jnp.einsum('eti,etj->eij', out_factors.astype(jnp.float32), in_factors.astype(jnp.float32))
    grads = (grads * (1.0 / jnp.sqrt(jnp.float32(L)))).astype(jnp.bfloat16).reshape(EXAMPLES, ORDER)
    wide = grads.astype(jnp.float32)
    fisher = jnp.dot(wide.T, wide) * (1.0 / jnp.sqrt(jnp.float32(EXAMPLES)))
    return fisher
```

```python
import functools

import jax
import jax.numpy as jnp
from jax import lax
from jax.experimental import pallas as pl
from jax.experimental.pallas import tpu as pltpu
from jax.sharding import PartitionSpec as P

L = 64
CORES = 2
MESH = pl.DeviceIdType.MESH
MIB = 1024 * 1024


def project_kernel(steps, lengths, act, og, w_in, w_out, in_f, out_f, in_acc, out_acc):
    step = pl.program_id(0)
    in_part = jnp.dot(act[...], w_in[...], preferred_element_type=jnp.float32)
    out_part = jnp.dot(og[...], w_out[...], preferred_element_type=jnp.float32)

    @pl.when(step == 0)
    def _():
        in_acc[...] = in_part
        out_acc[...] = out_part

    @pl.when(step > 0)
    def _():
        in_acc[...] += in_part
        out_acc[...] += out_part

    @pl.when(step == steps - 1)
    def _():
        in_f[...] = in_acc[...].astype(in_f.dtype)
        place = lax.broadcasted_iota(jnp.int32, (L, out_f.shape[1]), 0)
        for e in range(out_f.shape[0] // L):
            rows = pl.ds(e * L, L)
            kept = jnp.where(place < lengths[e], out_acc[rows, :], 0.0)
            out_f[rows, :] = kept.astype(out_f.dtype)


def project(activations, out_grads, lengths, proj_in, proj_out):
    steps = 4
    tokens, width = activations.shape[0], proj_in.shape[1]
    deep_in, deep_out = activations.shape[1] // steps, out_grads.shape[1] // steps
    factors = jax.ShapeDtypeStruct((tokens, width), jnp.bfloat16)
    whole = pl.BlockSpec((tokens, width), lambda s: (0, 0))
    return pl.pallas_call(
        functools.partial(project_kernel, steps),
        grid=(steps,),
        in_specs=[
            pl.BlockSpec(memory_space=pltpu.SMEM),
            pl.BlockSpec((tokens, deep_in), lambda s: (0, s)),
            pl.BlockSpec((tokens, deep_out), lambda s: (0, s)),
            pl.BlockSpec((deep_in, width), lambda s: (s, 0)),
            pl.BlockSpec((deep_out, width), lambda s: (s, 0)),
        ],
        out_specs=[whole, whole],
        out_shape=[factors, factors],
        scratch_shapes=[pltpu.VMEM((tokens, width), jnp.float32)] * 2,
        compiler_params=pltpu.CompilerParams(vmem_limit_bytes=32 * MIB),
    )(lengths, activations, out_grads, proj_in, proj_out)


def exchange_kernel(
    n, in_f, out_f, row_ref, col_ref,
    in_peer, out_peer, wide, blocks,
    peer_s, peer_r, c1_s, c1_r, r1_s, r1_r, r2_s, r2_r, c2_s, c2_r, fw_s, fw_r, own_s,
):
    r, c = lax.axis_index("row"), lax.axis_index("col")
    k, m = r // CORES, r % CORES
    peer = (k * CORES + 1 - m, c)
    width = in_f.shape[1]
    local_ex = in_f.shape[0] // L
    pair_ex = CORES * local_ex
    per_block = blocks.shape[2] // width

    def turn(start, d):
        return lax.rem(start + d + n, n)

    def send(src, dst, s, t, who):
        copy = pltpu.make_async_remote_copy(
            src_ref=src, dst_ref=dst, send_sem=s, recv_sem=t, device_id=who, device_id_type=MESH
        )
        copy.start()
        return copy

    barrier = pltpu.get_barrier_semaphore()
    pl.semaphore_signal(barrier, inc=1, device_id=peer, device_id_type=MESH)
    for d in range(1, n):
        pl.semaphore_signal(barrier, inc=1, device_id=(turn(k, d) * CORES + m, c), device_id_type=MESH)
        pl.semaphore_signal(barrier, inc=1, device_id=(r, turn(c, d)), device_id_type=MESH)
    pl.semaphore_wait(barrier, 2 * n - 1)

    swaps = [
        send(in_f, in_peer, peer_s.at[0], peer_r.at[0], peer),
        send(out_f, out_peer, peer_s.at[1], peer_r.at[1], peer),
    ]

    def outer(ins, outs, core):
        for e in range(local_ex):
            rows = pl.ds(e * L, L)
            grad = lax.dot_general(
                outs[rows, :], ins[rows, :], (((0,), (0,)), ((), ())), preferred_element_type=jnp.float32
            )
            place = pl.multiple_of((core * local_ex + e) * width, width)
            wide[pl.ds(place, width), :] = grad * (1.0 / jnp.sqrt(jnp.float32(L)))

    outer(in_f, out_f, m)
    for copy in swaps:
        copy.wait()
    outer(in_peer, out_peer, 1 - m)

    for q in range(n):
        for i in range(per_block):
            first = (q * CORES + m) * per_block + i
            blocks[q, :, i * width : (i + 1) * width] = wide[
                pl.ds(first, pair_ex, stride=width), :
            ].astype(blocks.dtype)

    to_col, to_row = [], []
    for d in range(1, n):
        q = turn(c, d)
        to_col.append(send(blocks.at[q], col_ref.at[m, c, k], c1_s.at[d], c1_r.at[d], (r, q)))
        q = turn(k, d)
        to_row.append(send(blocks.at[q], row_ref.at[c, k], r1_s.at[d], r1_r.at[d], (q * CORES + m, c)))
    own = [
        pltpu.make_async_copy(blocks.at[k], row_ref.at[c, k], own_s.at[0]),
        pltpu.make_async_copy(blocks.at[c], col_ref.at[m, c, k], own_s.at[1]),
    ]
    for copy in own:
        copy.start()

    for copy in to_row:
        copy.wait()
    own[0].wait()
    along = [
        send(row_ref.at[c], row_ref.at[c], r2_s.at[d], r2_r.at[d], (r, turn(c, d)))
        for d in range(1, n)
    ]

    for copy in to_col:
        copy.wait()
    own[1].wait()
    mine = col_ref.at[m, :, k]
    across = [
        send(mine, mine, c2_s.at[d], c2_r.at[d], (turn(k, d) * CORES + m, c)) for d in range(1, n)
    ]
    passed = [send(mine, mine, fw_s.at[0], fw_r.at[0], peer)]
    for d in range(1, n):
        across[d - 1].wait_recv()
        piece = col_ref.at[m, :, turn(k, -d)]
        passed.append(send(piece, piece, fw_s.at[d], fw_r.at[d], peer))
    for copy in across:
        copy.wait_send()
    for copy in along:
        copy.wait()
    for copy in passed:
        copy.wait()


def exchange(in_f, out_f, n_row, n_col):
    n = n_col
    assert n_row == CORES * n
    tokens, width = in_f.shape
    pair_ex = CORES * (tokens // L)
    block = width * width // n_row
    dma = pltpu.SemaphoreType.DMA
    anywhere = pl.BlockSpec(memory_space=pl.ANY)
    return pl.pallas_call(
        functools.partial(exchange_kernel, n),
        in_specs=[pl.BlockSpec(memory_space=pltpu.VMEM)] * 2,
        out_specs=[anywhere, anywhere],
        out_shape=[
            jax.ShapeDtypeStruct((n, n, pair_ex, block), jnp.bfloat16),
            jax.ShapeDtypeStruct((CORES, n, n, pair_ex, block), jnp.bfloat16),
        ],
        scratch_shapes=[
            pltpu.VMEM((tokens, width), jnp.bfloat16),
            pltpu.VMEM((tokens, width), jnp.bfloat16),
            pltpu.VMEM((pair_ex * width, width), jnp.float32),
            pltpu.VMEM((n, pair_ex, block), jnp.bfloat16),
            dma((2,)), dma((2,)),
        ]
        + [dma((n,))] * 10
        + [dma((2,))],
        compiler_params=pltpu.CompilerParams(
            collective_id=0, has_side_effects=True, vmem_limit_bytes=32 * MIB
        ),
    )(in_f, out_f)


def fisher_kernel(scale, left, right, out):
    out[...] = scale * lax.dot_general(
        left[...], right[0], (((0,), (0,)), ((), ())), preferred_element_type=jnp.float32
    )


def fisher(row_all, col_all):
    total, rows = row_all.shape
    halves, _, block = col_all.shape
    tile = min(256, rows)
    return pl.pallas_call(
        functools.partial(fisher_kernel, 1.0 / total**0.5),
        grid=(halves, rows // tile),
        in_specs=[
            pl.BlockSpec((total, tile), lambda h, i: (0, i)),
            pl.BlockSpec((1, total, block), lambda h, i: (h, 0, 0)),
        ],
        out_specs=pl.BlockSpec((tile, block), lambda h, i: (i, h)),
        out_shape=jax.ShapeDtypeStruct((rows, halves * block), jnp.float32),
        compiler_params=pltpu.CompilerParams(vmem_limit_bytes=32 * MIB),
    )(row_all, col_all)


def on_device(activations, out_grads, lengths, proj_in, proj_out):
    tokens = activations.shape[0] * L
    n_row = lax.axis_size("row")
    n_col = lax.axis_size("col")
    in_f, out_f = project(
        activations.reshape(tokens, -1), out_grads.reshape(tokens, -1), lengths, proj_in, proj_out
    )
    row_all, col_all = exchange(in_f, out_f, n_row, n_col)
    block = row_all.shape[-1]
    return fisher(row_all.reshape(-1, block), col_all.reshape(CORES, -1, block))


def solution(mesh):
    placed = (
        P(("row", "col"), None, None),
        P(("row", "col"), None, None),
        P(("row", "col")),
        P(),
        P(),
    )
    return jax.shard_map(
        on_device, mesh=mesh, in_specs=placed, out_specs=P("row", "col"), check_vma=False
    )
```

```python
import functools

import jax
import jax.numpy as jnp
from jax import lax
from jax.experimental import pallas as pl
from jax.experimental.pallas import tpu as pltpu
from jax.sharding import PartitionSpec as P

L = 64
CORES = 2
MESH = pl.DeviceIdType.MESH
MIB = 1024 * 1024


def project_kernel(steps, lengths, act, og, w_in, w_out, in_f, out_f, in_acc, out_acc):
    step = pl.program_id(0)
    in_part = jnp.dot(act[...], w_in[...], preferred_element_type=jnp.float32)
    out_part = jnp.dot(og[...], w_out[...], preferred_element_type=jnp.float32)

    @pl.when(step == 0)
    def _():
        in_acc[...] = in_part
        out_acc[...] = out_part

    @pl.when(step > 0)
    def _():
        in_acc[...] += in_part
        out_acc[...] += out_part

    @pl.when(step == steps - 1)
    def _():
        in_f[...] = in_acc[...].astype(in_f.dtype)
        place = lax.broadcasted_iota(jnp.int32, (L, out_f.shape[1]), 0)
        for e in range(out_f.shape[0] // L):
            rows = pl.ds(e * L, L)
            kept = jnp.where(place < lengths[e], out_acc[rows, :], 0.0)
            out_f[rows, :] = kept.astype(out_f.dtype)


def project(activations, out_grads, lengths, proj_in, proj_out):
    steps = 4
    tokens, width = activations.shape[0], proj_in.shape[1]
    deep_in, deep_out = activations.shape[1] // steps, out_grads.shape[1] // steps
    factors = jax.ShapeDtypeStruct((tokens, width), jnp.bfloat16)
    whole = pl.BlockSpec((tokens, width), lambda s: (0, 0))
    return pl.pallas_call(
        functools.partial(project_kernel, steps),
        grid=(steps,),
        in_specs=[
            pl.BlockSpec(memory_space=pltpu.SMEM),
            pl.BlockSpec((tokens, deep_in), lambda s: (0, s)),
            pl.BlockSpec((tokens, deep_out), lambda s: (0, s)),
            pl.BlockSpec((deep_in, width), lambda s: (s, 0)),
            pl.BlockSpec((deep_out, width), lambda s: (s, 0)),
        ],
        out_specs=[whole, whole],
        out_shape=[factors, factors],
        scratch_shapes=[pltpu.VMEM((tokens, width), jnp.float32)] * 2,
        compiler_params=pltpu.CompilerParams(vmem_limit_bytes=60 * MIB),
    )(lengths, activations, out_grads, proj_in, proj_out)


def exchange_kernel(
    n, in_f, out_f, row_ref, col_ref,
    in_peer, out_peer, wide, blocks,
    peer_s, peer_r, c1_s, c1_r, r1_s, r1_r, line_s, line_r, c2_s, c2_r, fw_s, fw_r, own_s,
):
    r, c = lax.axis_index("row"), lax.axis_index("col")
    k, m = r // CORES, r % CORES
    peer = (k * CORES + 1 - m, c)
    width = in_f.shape[1]
    local_ex = in_f.shape[0] // L
    pair_ex = CORES * local_ex
    per_block = blocks.shape[2] // width

    def turn(start, d):
        return lax.rem(start + d + n, n)

    def send(src, dst, s, t, who):
        copy = pltpu.make_async_remote_copy(
            src_ref=src, dst_ref=dst, send_sem=s, recv_sem=t, device_id=who, device_id_type=MESH
        )
        copy.start()
        return copy

    barrier = pltpu.get_barrier_semaphore()
    pl.semaphore_signal(barrier, inc=1, device_id=peer, device_id_type=MESH)
    for d in range(1, n):
        pl.semaphore_signal(barrier, inc=1, device_id=(turn(k, d) * CORES + m, c), device_id_type=MESH)
        pl.semaphore_signal(barrier, inc=1, device_id=(r, turn(c, d)), device_id_type=MESH)
    pl.semaphore_wait(barrier, 2 * n - 1)

    swaps = [
        send(in_f, in_peer, peer_s.at[0], peer_r.at[0], peer),
        send(out_f, out_peer, peer_s.at[1], peer_r.at[1], peer),
    ]

    def outer(ins, outs, core):
        for e in range(local_ex):
            rows = pl.ds(e * L, L)
            grad = lax.dot_general(
                outs[rows, :], ins[rows, :], (((0,), (0,)), ((), ())), preferred_element_type=jnp.float32
            )
            place = pl.multiple_of((core * local_ex + e) * width, width)
            wide[pl.ds(place, width), :] = grad * (1.0 / jnp.sqrt(jnp.float32(L)))

    outer(in_f, out_f, m)
    for copy in swaps:
        copy.wait()
    outer(in_peer, out_peer, 1 - m)

    for q in range(n):
        for i in range(per_block):
            first = (q * CORES + m) * per_block + i
            blocks[q, :, i * width : (i + 1) * width] = wide[
                pl.ds(first, pair_ex, stride=width), :
            ].astype(blocks.dtype)

    to_col, to_row = [], []
    for d in range(1, n):
        q = turn(c, d)
        to_col.append(send(blocks.at[q], col_ref.at[m, c, k], c1_s.at[d], c1_r.at[d], (r, q)))
        q = turn(k, d)
        to_row.append(send(blocks.at[q], row_ref.at[c, k], r1_s.at[d], r1_r.at[d], (q * CORES + m, c)))
    own = [
        pltpu.make_async_copy(blocks.at[k], row_ref.at[c, k], own_s.at[0]),
        pltpu.make_async_copy(blocks.at[c], col_ref.at[m, c, k], own_s.at[1]),
    ]
    for copy in own:
        copy.start()

    half = n // 2

    def hop(way, t, p):
        shard = row_ref.at[c - way * t, pl.ds(p * half, half)]
        w = (way + 1) // 2
        return pltpu.make_async_remote_copy(
            src_ref=shard,
            dst_ref=shard,
            send_sem=line_s.at[w, t, p],
            recv_sem=line_r.at[w, t, p],
            device_id=(r, c + way),
            device_id_type=MESH,
        )

    def arrival(way, t, p):
        shard = row_ref.at[c - way * t, pl.ds(p * half, half)]
        w = (way + 1) // 2
        return pltpu.make_async_remote_copy(
            src_ref=shard,
            dst_ref=shard,
            send_sem=line_s.at[w, t - 1, p],
            recv_sem=line_r.at[w, t - 1, p],
            device_id=(r, c - way),
            device_id_type=MESH,
        )

    def comes(way, t):
        return c - t >= 0 if way > 0 else c + t <= n - 1

    def goes(way):
        return c <= n - 2 if way > 0 else c >= 1

    def relay(t):
        for p in range(2):
            for way in (1, -1):
                if t > 0:

                    @pl.when(comes(way, t))
                    def _(way=way, p=p):
                        arrival(way, t, p).wait_recv()

                if t < n - 1:

                    @pl.when(jnp.logical_and(comes(way, t), goes(way)))
                    def _(way=way, p=p):
                        hop(way, t, p).start()

    for copy in to_row:
        copy.wait()
    own[0].wait()
    relay(0)

    for copy in to_col:
        copy.wait()
    own[1].wait()
    mine = col_ref.at[m, :, k]
    across = [
        send(mine, mine, c2_s.at[d], c2_r.at[d], (turn(k, d) * CORES + m, c)) for d in range(1, n)
    ]
    passed = [send(mine, mine, fw_s.at[0], fw_r.at[0], peer)]
    for d in range(1, n):
        relay(d)
        across[d - 1].wait_recv()
        piece = col_ref.at[m, :, turn(k, -d)]
        passed.append(send(piece, piece, fw_s.at[d], fw_r.at[d], peer))
    for copy in across:
        copy.wait_send()
    for t in range(n - 1):
        for way in (1, -1):

            @pl.when(jnp.logical_and(comes(way, t), goes(way)))
            def _(way=way, t=t):
                for p in range(2):
                    hop(way, t, p).wait_send()

    for copy in passed:
        copy.wait()


def exchange(in_f, out_f, n_row, n_col):
    n = n_col
    assert n_row == CORES * n
    tokens, width = in_f.shape
    pair_ex = CORES * (tokens // L)
    block = width * width // n_row
    dma = pltpu.SemaphoreType.DMA
    anywhere = pl.BlockSpec(memory_space=pl.ANY)
    return pl.pallas_call(
        functools.partial(exchange_kernel, n),
        in_specs=[pl.BlockSpec(memory_space=pltpu.VMEM)] * 2,
        out_specs=[anywhere, anywhere],
        out_shape=[
            jax.ShapeDtypeStruct((n, n, pair_ex, block), jnp.bfloat16),
            jax.ShapeDtypeStruct((CORES, n, n, pair_ex, block), jnp.bfloat16),
        ],
        scratch_shapes=[
            pltpu.VMEM((tokens, width), jnp.bfloat16),
            pltpu.VMEM((tokens, width), jnp.bfloat16),
            pltpu.VMEM((pair_ex * width, width), jnp.float32),
            pltpu.VMEM((n, pair_ex, block), jnp.bfloat16),
            dma((2,)), dma((2,)),
        ]
        + [dma((n,))] * 4
        + [dma((2, n - 1, 2))] * 2
        + [dma((n,))] * 4
        + [dma((2,))],
        compiler_params=pltpu.CompilerParams(
            collective_id=0, has_side_effects=True, vmem_limit_bytes=32 * MIB
        ),
    )(in_f, out_f)


def fisher_kernel(scale, slots, parts, left, right, out, held, sems):
    h, i = pl.program_id(0), pl.program_id(1)
    tiles = pl.num_programs(1)
    steps = pl.num_programs(0) * tiles
    step = h * tiles + i
    _, tile, block = held.shape
    piece = tile // parts

    def writes(s):
        slot = lax.rem(s, slots)
        top, side = lax.rem(s, tiles) * tile, lax.div(s, tiles) * block
        return [
            pltpu.make_async_copy(
                held.at[slot, pl.ds(p * piece, piece)],
                out.at[pl.ds(top + p * piece, piece), pl.ds(pl.multiple_of(side, block), block)],
                sems.at[slot, p],
            )
            for p in range(parts)
        ]

    @pl.when(step >= slots)
    def _():
        for copy in writes(step - slots):
            copy.wait()

    slot = lax.rem(step, slots)
    held[slot] = scale * lax.dot_general(
        left[...], right[0], (((0,), (0,)), ((), ())), preferred_element_type=jnp.float32
    )
    for copy in writes(step):
        copy.start()

    @pl.when(step == steps - 1)
    def _():
        for back in range(slots - 1, -1, -1):
            for copy in writes(step - back):
                copy.wait()


def fisher(row_all, col_all):
    total, rows = row_all.shape
    halves, _, block = col_all.shape
    tile, slots, parts = min(256, rows // 4), 4, 2
    return pl.pallas_call(
        functools.partial(fisher_kernel, 1.0 / total**0.5, slots, parts),
        grid=(halves, rows // tile),
        in_specs=[
            pl.BlockSpec((total, tile), lambda h, i: (0, i)),
            pl.BlockSpec((1, total, block), lambda h, i: (h, 0, 0)),
        ],
        out_specs=pl.BlockSpec(memory_space=pl.ANY),
        out_shape=jax.ShapeDtypeStruct((rows, halves * block), jnp.float32),
        scratch_shapes=[
            pltpu.VMEM((slots, tile, block), jnp.float32),
            pltpu.SemaphoreType.DMA((slots, parts)),
        ],
        compiler_params=pltpu.CompilerParams(vmem_limit_bytes=24 * MIB),
    )(row_all, col_all)


def on_device(activations, out_grads, lengths, proj_in, proj_out):
    tokens = activations.shape[0] * L
    n_row = lax.axis_size("row")
    n_col = lax.axis_size("col")
    in_f, out_f = project(
        activations.reshape(tokens, -1), out_grads.reshape(tokens, -1), lengths, proj_in, proj_out
    )
    row_all, col_all = exchange(in_f, out_f, n_row, n_col)
    block = row_all.shape[-1]
    return fisher(row_all.reshape(-1, block), col_all.reshape(CORES, -1, block))


def solution(mesh):
    placed = (
        P(("row", "col"), None, None),
        P(("row", "col"), None, None),
        P(("row", "col")),
        P(),
        P(),
    )
    return jax.shard_map(
        on_device, mesh=mesh, in_specs=placed, out_specs=P("row", "col"), check_vma=False
    )
```

```python
import functools
import math

import jax
import jax.numpy as jnp
from jax import lax
from jax.experimental import pallas as pl
from jax.experimental.pallas import tpu as pltpu
from jax.sharding import PartitionSpec as P

L = 64
CORES = 2
MESH = pl.DeviceIdType.MESH
MIB = 1024 * 1024


def exchange_kernel(
    n, lengths, act, og, w_in, w_out, row_ref, col_ref,
    act_v, og_v, w_in_v, w_out_v, in_acc, out_acc,
    in_f, out_f, in_peer, out_peer, wide, blocks,
    load_s, peer_s, peer_r, c1_s, c1_r, r1_s, r1_r, line_s, line_r, c2_s, c2_r, fw_s, fw_r, own_s,
):
    r, c = lax.axis_index("row"), lax.axis_index("col")
    k, m = r // CORES, r % CORES
    peer = (k * CORES + 1 - m, c)
    width = in_f.shape[1]
    local_ex = in_f.shape[0] // L
    pair_ex = CORES * local_ex
    per_block = blocks.shape[2] // width

    def loads(x, w, x_v, w_v, first):
        depth = x_v.shape[2]
        return [
            (
                pltpu.make_async_copy(x.at[:, pl.ds(q * depth, depth)], x_v.at[q], load_s.at[first + q, 0]),
                pltpu.make_async_copy(w.at[pl.ds(q * depth, depth)], w_v.at[q], load_s.at[first + q, 1]),
            )
            for q in range(x_v.shape[0])
        ]

    act_loads = loads(act, w_in, act_v, w_in_v, 0)
    og_loads = loads(og, w_out, og_v, w_out_v, len(act_loads))
    for pair in act_loads + og_loads:
        for copy in pair:
            copy.start()

    def project(pairs, x_v, w_v, acc):
        for q, pair in enumerate(pairs):
            for copy in pair:
                copy.wait()
            part = jnp.dot(x_v[q], w_v[q], preferred_element_type=jnp.float32)
            acc[...] = part if q == 0 else acc[...] + part

    def turn(start, d):
        return lax.rem(start + d + n, n)

    def send(src, dst, s, t, who):
        copy = pltpu.make_async_remote_copy(
            src_ref=src, dst_ref=dst, send_sem=s, recv_sem=t, device_id=who, device_id_type=MESH
        )
        copy.start()
        return copy

    barrier = pltpu.get_barrier_semaphore()
    pl.semaphore_signal(barrier, inc=1, device_id=peer, device_id_type=MESH)
    for d in range(1, n):
        pl.semaphore_signal(barrier, inc=1, device_id=(turn(k, d) * CORES + m, c), device_id_type=MESH)
        pl.semaphore_signal(barrier, inc=1, device_id=(r, turn(c, d)), device_id_type=MESH)

    project(act_loads, act_v, w_in_v, in_acc)
    in_f[...] = in_acc[...].astype(in_f.dtype)
    pl.semaphore_wait(barrier, 2 * n - 1)
    swaps = [send(in_f, in_peer, peer_s.at[0], peer_r.at[0], peer)]

    project(og_loads, og_v, w_out_v, out_acc)
    place = lax.broadcasted_iota(jnp.int32, (L, width), 0)
    for e in range(local_ex):
        rows = pl.ds(e * L, L)
        out_f[rows, :] = jnp.where(place < lengths[e], out_acc[rows, :], 0.0).astype(out_f.dtype)
    swaps.append(send(out_f, out_peer, peer_s.at[1], peer_r.at[1], peer))

    def outer(ins, outs, core):
        for e in range(local_ex):
            rows = pl.ds(e * L, L)
            grad = lax.dot_general(
                outs[rows, :], ins[rows, :], (((0,), (0,)), ((), ())), preferred_element_type=jnp.float32
            )
            start = pl.multiple_of((core * local_ex + e) * width, width)
            wide[pl.ds(start, width), :] = grad * (1.0 / jnp.sqrt(jnp.float32(L)))

    outer(in_f, out_f, m)
    for copy in swaps:
        copy.wait()
    outer(in_peer, out_peer, 1 - m)

    for q in range(n):
        for i in range(per_block):
            first = (q * CORES + m) * per_block + i
            blocks[q, :, i * width : (i + 1) * width] = wide[
                pl.ds(first, pair_ex, stride=width), :
            ].astype(blocks.dtype)

    to_col, to_row = [], []
    for d in range(1, n):
        q = turn(c, d)
        to_col.append(send(blocks.at[q], col_ref.at[m, c, k], c1_s.at[d], c1_r.at[d], (r, q)))
        q = turn(k, d)
        to_row.append(send(blocks.at[q], row_ref.at[c, k], r1_s.at[d], r1_r.at[d], (q * CORES + m, c)))
    own = [
        pltpu.make_async_copy(blocks.at[k], row_ref.at[c, k], own_s.at[0]),
        pltpu.make_async_copy(blocks.at[c], col_ref.at[m, c, k], own_s.at[1]),
    ]
    for copy in own:
        copy.start()

    half = n // 2

    def hop(way, t, p):
        shard = row_ref.at[c - way * t, pl.ds(p * half, half)]
        w = (way + 1) // 2
        return pltpu.make_async_remote_copy(
            src_ref=shard,
            dst_ref=shard,
            send_sem=line_s.at[w, t, p],
            recv_sem=line_r.at[w, t, p],
            device_id=(r, c + way),
            device_id_type=MESH,
        )

    def arrival(way, t, p):
        shard = row_ref.at[c - way * t, pl.ds(p * half, half)]
        w = (way + 1) // 2
        return pltpu.make_async_remote_copy(
            src_ref=shard,
            dst_ref=shard,
            send_sem=line_s.at[w, t - 1, p],
            recv_sem=line_r.at[w, t - 1, p],
            device_id=(r, c - way),
            device_id_type=MESH,
        )

    def comes(way, t):
        return c - t >= 0 if way > 0 else c + t <= n - 1

    def goes(way):
        return c <= n - 2 if way > 0 else c >= 1

    def relay(t):
        for p in range(2):
            for way in (1, -1):
                if t > 0:

                    @pl.when(comes(way, t))
                    def _(way=way, p=p):
                        arrival(way, t, p).wait_recv()

                if t < n - 1:

                    @pl.when(jnp.logical_and(comes(way, t), goes(way)))
                    def _(way=way, p=p):
                        hop(way, t, p).start()

    for copy in to_row:
        copy.wait()
    own[0].wait()
    relay(0)

    for copy in to_col:
        copy.wait()
    own[1].wait()
    mine = col_ref.at[m, :, k]
    across = [
        send(mine, mine, c2_s.at[d], c2_r.at[d], (turn(k, d) * CORES + m, c)) for d in range(1, n)
    ]
    passed = [send(mine, mine, fw_s.at[0], fw_r.at[0], peer)]
    for d in range(1, n):
        relay(d)
        across[d - 1].wait_recv()
        piece = col_ref.at[m, :, turn(k, -d)]
        passed.append(send(piece, piece, fw_s.at[d], fw_r.at[d], peer))
    for copy in across:
        copy.wait_send()
    for t in range(n - 1):
        for way in (1, -1):

            @pl.when(jnp.logical_and(comes(way, t), goes(way)))
            def _(way=way, t=t):
                for p in range(2):
                    hop(way, t, p).wait_send()

    for copy in passed:
        copy.wait()


def exchange(activations, out_grads, lengths, proj_in, proj_out, n_row, n_col):
    n = n_col
    assert n_row == CORES * n
    tokens, width = activations.shape[0], proj_in.shape[1]
    pair_ex = CORES * (tokens // L)
    block = width * width // n_row
    depth = math.gcd(proj_in.shape[0], proj_out.shape[0])
    ins, outs = proj_in.shape[0] // depth, proj_out.shape[0] // depth
    dma = pltpu.SemaphoreType.DMA
    anywhere = pl.BlockSpec(memory_space=pl.ANY)
    return pl.pallas_call(
        functools.partial(exchange_kernel, n),
        in_specs=[pl.BlockSpec(memory_space=pltpu.SMEM)] + [anywhere] * 4,
        out_specs=[anywhere, anywhere],
        out_shape=[
            jax.ShapeDtypeStruct((n, n, pair_ex, block), jnp.bfloat16),
            jax.ShapeDtypeStruct((CORES, n, n, pair_ex, block), jnp.bfloat16),
        ],
        scratch_shapes=[
            pltpu.VMEM((ins, tokens, depth), jnp.bfloat16),
            pltpu.VMEM((outs, tokens, depth), jnp.bfloat16),
            pltpu.VMEM((ins, depth, width), jnp.bfloat16),
            pltpu.VMEM((outs, depth, width), jnp.bfloat16),
        ]
        + [pltpu.VMEM((tokens, width), jnp.float32)] * 2
        + [pltpu.VMEM((tokens, width), jnp.bfloat16)] * 4
        + [
            pltpu.VMEM((pair_ex * width, width), jnp.float32),
            pltpu.VMEM((n, pair_ex, block), jnp.bfloat16),
            dma((ins + outs, 2)),
            dma((2,)), dma((2,)),
        ]
        + [dma((n,))] * 4
        + [dma((2, n - 1, 2))] * 2
        + [dma((n,))] * 4
        + [dma((2,))],
        compiler_params=pltpu.CompilerParams(
            collective_id=0, has_side_effects=True, vmem_limit_bytes=58 * MIB
        ),
    )(lengths, activations, out_grads, proj_in, proj_out)


def fisher_kernel(scale, slots, parts, left, right, out, held, sems):
    h, i = pl.program_id(0), pl.program_id(1)
    tiles = pl.num_programs(1)
    steps = pl.num_programs(0) * tiles
    step = h * tiles + i
    _, tile, block = held.shape
    piece = tile // parts

    def writes(s):
        slot = lax.rem(s, slots)
        top, side = lax.rem(s, tiles) * tile, lax.div(s, tiles) * block
        return [
            pltpu.make_async_copy(
                held.at[slot, pl.ds(p * piece, piece)],
                out.at[pl.ds(top + p * piece, piece), pl.ds(pl.multiple_of(side, block), block)],
                sems.at[slot, p],
            )
            for p in range(parts)
        ]

    @pl.when(step >= slots)
    def _():
        for copy in writes(step - slots):
            copy.wait()

    slot = lax.rem(step, slots)
    held[slot] = scale * lax.dot_general(
        left[...], right[0], (((0,), (0,)), ((), ())), preferred_element_type=jnp.float32
    )
    for copy in writes(step):
        copy.start()

    @pl.when(step == steps - 1)
    def _():
        for back in range(slots - 1, -1, -1):
            for copy in writes(step - back):
                copy.wait()


def fisher(row_all, col_all):
    total, rows = row_all.shape
    halves, _, block = col_all.shape
    tile, slots, parts = min(256, rows // 4), 4, 2
    return pl.pallas_call(
        functools.partial(fisher_kernel, 1.0 / total**0.5, slots, parts),
        grid=(halves, rows // tile),
        in_specs=[
            pl.BlockSpec((total, tile), lambda h, i: (0, i)),
            pl.BlockSpec((1, total, block), lambda h, i: (h, 0, 0)),
        ],
        out_specs=pl.BlockSpec(memory_space=pl.ANY),
        out_shape=jax.ShapeDtypeStruct((rows, halves * block), jnp.float32),
        scratch_shapes=[
            pltpu.VMEM((slots, tile, block), jnp.float32),
            pltpu.SemaphoreType.DMA((slots, parts)),
        ],
        compiler_params=pltpu.CompilerParams(vmem_limit_bytes=60 * MIB),
    )(row_all, col_all)


def on_device(activations, out_grads, lengths, proj_in, proj_out):
    tokens = activations.shape[0] * L
    n_row = lax.axis_size("row")
    n_col = lax.axis_size("col")
    row_all, col_all = exchange(
        activations.reshape(tokens, -1),
        out_grads.reshape(tokens, -1),
        lengths, proj_in, proj_out, n_row, n_col,
    )
    block = row_all.shape[-1]
    return fisher(row_all.reshape(-1, block), col_all.reshape(CORES, -1, block))


def solution(mesh):
    placed = (
        P(("row", "col"), None, None),
        P(("row", "col"), None, None),
        P(("row", "col")),
        P(),
        P(),
    )
    return jax.shard_map(
        on_device, mesh=mesh, in_specs=placed, out_specs=P("row", "col"), check_vma=False
    )
```

```python
import functools
import math

import jax
import jax.numpy as jnp
from jax import lax
from jax.experimental import pallas as pl
from jax.experimental.pallas import tpu as pltpu
from jax.sharding import PartitionSpec as P

L = 64
CORES = 2
MESH = pl.DeviceIdType.MESH
MIB = 1024 * 1024


def exchange_kernel(
    n, lengths, act, og, w_in, w_out, row_ref, col_ref,
    act_v, og_v, w_in_v, w_out_v, in_acc, out_acc,
    in_f, out_f, in_peer, out_peer, wide, blocks,
    load_s, peer_s, peer_r, c1_s, c1_r, r1_s, r1_r, line_s, line_r, c2_s, c2_r, fw_s, fw_r, own_s,
):
    r, c = lax.axis_index("row"), lax.axis_index("col")
    k, m = r // CORES, r % CORES
    peer = (k * CORES + 1 - m, c)
    width = in_f.shape[1]
    local_ex = in_f.shape[0] // L
    pair_ex = CORES * local_ex
    per_block = blocks.shape[2] // width

    def loads(x, w, x_v, w_v, first):
        depth = x_v.shape[2]
        return [
            (
                pltpu.make_async_copy(x.at[:, pl.ds(q * depth, depth)], x_v.at[q], load_s.at[first + q, 0]),
                pltpu.make_async_copy(w.at[pl.ds(q * depth, depth)], w_v.at[q], load_s.at[first + q, 1]),
            )
            for q in range(x_v.shape[0])
        ]

    act_loads = loads(act, w_in, act_v, w_in_v, 0)
    og_loads = loads(og, w_out, og_v, w_out_v, len(act_loads))
    for pair in act_loads + og_loads:
        for copy in pair:
            copy.start()

    def project(pairs, x_v, w_v, acc):
        for q, pair in enumerate(pairs):
            for copy in pair:
                copy.wait()
            part = jnp.dot(x_v[q], w_v[q], preferred_element_type=jnp.float32)
            acc[...] = part if q == 0 else acc[...] + part

    def turn(start, d):
        return lax.rem(start + d + n, n)

    def send(src, dst, s, t, who):
        copy = pltpu.make_async_remote_copy(
            src_ref=src, dst_ref=dst, send_sem=s, recv_sem=t, device_id=who, device_id_type=MESH
        )
        copy.start()
        return copy

    barrier = pltpu.get_barrier_semaphore()
    pl.semaphore_signal(barrier, inc=1, device_id=peer, device_id_type=MESH)
    for d in range(1, n):
        pl.semaphore_signal(barrier, inc=1, device_id=(turn(k, d) * CORES + m, c), device_id_type=MESH)
        pl.semaphore_signal(barrier, inc=1, device_id=(r, turn(c, d)), device_id_type=MESH)

    project(act_loads, act_v, w_in_v, in_acc)
    in_f[...] = in_acc[...].astype(in_f.dtype)
    pl.semaphore_wait(barrier, 2 * n - 1)
    swaps = [send(in_f, in_peer, peer_s.at[0], peer_r.at[0], peer)]

    project(og_loads, og_v, w_out_v, out_acc)
    place = lax.broadcasted_iota(jnp.int32, (L, width), 0)
    for e in range(local_ex):
        rows = pl.ds(e * L, L)
        out_f[rows, :] = jnp.where(place < lengths[e], out_acc[rows, :], 0.0).astype(out_f.dtype)
    swaps.append(send(out_f, out_peer, peer_s.at[1], peer_r.at[1], peer))

    def outer(ins, outs, core):
        for e in range(local_ex):
            rows = pl.ds(e * L, L)
            grad = lax.dot_general(
                outs[rows, :], ins[rows, :], (((0,), (0,)), ((), ())), preferred_element_type=jnp.float32
            )
            start = pl.multiple_of((core * local_ex + e) * width, width)
            wide[pl.ds(start, width), :] = grad * (1.0 / jnp.sqrt(jnp.float32(L)))

    outer(in_f, out_f, m)
    for copy in swaps:
        copy.wait()
    outer(in_peer, out_peer, 1 - m)

    for q in range(n):
        for i in range(per_block):
            first = (q * CORES + m) * per_block + i
            blocks[q, :, i * width : (i + 1) * width] = wide[
                pl.ds(first, pair_ex, stride=width), :
            ].astype(blocks.dtype)

    to_col, to_row = [], []
    for d in range(1, n):
        q = turn(c, d)
        to_col.append(send(blocks.at[q], col_ref.at[m, c, k], c1_s.at[d], c1_r.at[d], (r, q)))
        q = turn(k, d)
        to_row.append(send(blocks.at[q], row_ref.at[c, k], r1_s.at[d], r1_r.at[d], (q * CORES + m, c)))
    own = [
        pltpu.make_async_copy(blocks.at[k], row_ref.at[c, k], own_s.at[0]),
        pltpu.make_async_copy(blocks.at[c], col_ref.at[m, c, k], own_s.at[1]),
    ]
    for copy in own:
        copy.start()

    half = n // 2

    def hop(way, t, p):
        shard = row_ref.at[c - way * t, pl.ds(p * half, half)]
        w = (way + 1) // 2
        return pltpu.make_async_remote_copy(
            src_ref=shard,
            dst_ref=shard,
            send_sem=line_s.at[w, t, p],
            recv_sem=line_r.at[w, t, p],
            device_id=(r, c + way),
            device_id_type=MESH,
        )

    def arrival(way, t, p):
        shard = row_ref.at[c - way * t, pl.ds(p * half, half)]
        w = (way + 1) // 2
        return pltpu.make_async_remote_copy(
            src_ref=shard,
            dst_ref=shard,
            send_sem=line_s.at[w, t - 1, p],
            recv_sem=line_r.at[w, t - 1, p],
            device_id=(r, c - way),
            device_id_type=MESH,
        )

    def comes(way, t):
        return c - t >= 0 if way > 0 else c + t <= n - 1

    def goes(way):
        return c <= n - 2 if way > 0 else c >= 1

    def relay(t):
        for p in range(2):
            for way in (1, -1):
                if t > 0:

                    @pl.when(comes(way, t))
                    def _(way=way, p=p):
                        arrival(way, t, p).wait_recv()

                if t < n - 1:

                    @pl.when(jnp.logical_and(comes(way, t), goes(way)))
                    def _(way=way, p=p):
                        hop(way, t, p).start()

    for copy in to_row:
        copy.wait()
    own[0].wait()
    relay(0)

    for copy in to_col:
        copy.wait()
    own[1].wait()
    mine = col_ref.at[m, :, k]
    across = [
        send(mine, mine, c2_s.at[d], c2_r.at[d], (turn(k, d) * CORES + m, c)) for d in range(1, n)
    ]
    passed = [send(mine, mine, fw_s.at[0], fw_r.at[0], peer)]
    for t in range(1, n - 1):
        relay(t)
    for d in range(1, n):
        across[d - 1].wait_recv()
        piece = col_ref.at[m, :, turn(k, -d)]
        passed.append(send(piece, piece, fw_s.at[d], fw_r.at[d], peer))
    relay(n - 1)
    for copy in across:
        copy.wait_send()
    for t in range(n - 1):
        for way in (1, -1):

            @pl.when(jnp.logical_and(comes(way, t), goes(way)))
            def _(way=way, t=t):
                for p in range(2):
                    hop(way, t, p).wait_send()

    for copy in passed:
        copy.wait()


def exchange(activations, out_grads, lengths, proj_in, proj_out, n_row, n_col):
    n = n_col
    assert n_row == CORES * n
    tokens, width = activations.shape[0], proj_in.shape[1]
    pair_ex = CORES * (tokens // L)
    block = width * width // n_row
    depth = math.gcd(proj_in.shape[0], proj_out.shape[0])
    ins, outs = proj_in.shape[0] // depth, proj_out.shape[0] // depth
    dma = pltpu.SemaphoreType.DMA
    return pl.pallas_call(
        functools.partial(exchange_kernel, n),
        in_specs=[pl.BlockSpec(memory_space=pltpu.SMEM)] + [pl.BlockSpec(memory_space=pl.ANY)] * 4,
        out_specs=[pl.BlockSpec(memory_space=pl.ANY)] * 2,
        out_shape=[
            jax.ShapeDtypeStruct((n, n, pair_ex, block), jnp.bfloat16),
            jax.ShapeDtypeStruct((CORES, n, n, pair_ex, block), jnp.bfloat16),
        ],
        scratch_shapes=[
            pltpu.VMEM((ins, tokens, depth), jnp.bfloat16),
            pltpu.VMEM((outs, tokens, depth), jnp.bfloat16),
            pltpu.VMEM((ins, depth, width), jnp.bfloat16),
            pltpu.VMEM((outs, depth, width), jnp.bfloat16),
        ]
        + [pltpu.VMEM((tokens, width), jnp.float32)] * 2
        + [pltpu.VMEM((tokens, width), jnp.bfloat16)] * 4
        + [
            pltpu.VMEM((pair_ex * width, width), jnp.float32),
            pltpu.VMEM((n, pair_ex, block), jnp.bfloat16),
            dma((ins + outs, 2)),
            dma((2,)), dma((2,)),
        ]
        + [dma((n,))] * 4
        + [dma((2, n - 1, 2))] * 2
        + [dma((n,))] * 4
        + [dma((2,))],
        compiler_params=pltpu.CompilerParams(
            collective_id=0, has_side_effects=True, vmem_limit_bytes=58 * MIB
        ),
    )(lengths, activations, out_grads, proj_in, proj_out)


def fisher_kernel(scale, slots, parts, left_h, right_h, out, left, right, held, sems, load_s):
    h, i = pl.program_id(0), pl.program_id(1)
    tiles = pl.num_programs(1)
    steps = pl.num_programs(0) * tiles
    step = h * tiles + i
    _, tile, block = held.shape
    piece = tile // parts

    def writes(s):
        slot = lax.rem(s, slots)
        top, side = lax.rem(s, tiles) * tile, lax.div(s, tiles) * block
        return [
            pltpu.make_async_copy(
                held.at[slot, pl.ds(p * piece, piece)],
                out.at[pl.ds(top + p * piece, piece), pl.ds(pl.multiple_of(side, block), block)],
                sems.at[slot, p],
            )
            for p in range(parts)
        ]

    loads = [pltpu.make_async_copy(left_h, left, load_s.at[0])] + [
        pltpu.make_async_copy(right_h.at[s], right.at[s], load_s.at[1 + s]) for s in range(CORES)
    ]

    @pl.when(step == 0)
    def _():
        for copy in loads:
            copy.start()
        loads[0].wait()

    for s in range(CORES):

        @pl.when(step == s * tiles)
        def _(s=s):
            loads[1 + s].wait()

    @pl.when(step >= slots)
    def _():
        for copy in writes(step - slots):
            copy.wait()

    slot = lax.rem(step, slots)
    held[slot] = scale * lax.dot_general(
        left[:, pl.ds(pl.multiple_of(i * tile, tile), tile)], right[h], (((0,), (0,)), ((), ())), preferred_element_type=jnp.float32
    )
    for copy in writes(step):
        copy.start()

    @pl.when(step == steps - 1)
    def _():
        for back in range(slots - 1, -1, -1):
            for copy in writes(step - back):
                copy.wait()


def fisher(row_all, col_all):
    total, rows = row_all.shape
    halves, _, block = col_all.shape
    tile, slots, parts = min(256, rows // 4), 4, 2
    return pl.pallas_call(
        functools.partial(fisher_kernel, 1.0 / total**0.5, slots, parts),
        grid=(halves, rows // tile),
        in_specs=[
            pl.BlockSpec(memory_space=pl.ANY),
            pl.BlockSpec(memory_space=pl.ANY),
        ],
        out_specs=pl.BlockSpec(memory_space=pl.ANY),
        out_shape=jax.ShapeDtypeStruct((rows, halves * block), jnp.float32),
        scratch_shapes=[
            pltpu.VMEM(row_all.shape, row_all.dtype),
            pltpu.VMEM(col_all.shape, col_all.dtype),
            pltpu.VMEM((slots, tile, block), jnp.float32),
            pltpu.SemaphoreType.DMA((slots, parts)),
            pltpu.SemaphoreType.DMA((1 + halves,)),
        ],
        compiler_params=pltpu.CompilerParams(vmem_limit_bytes=60 * MIB),
    )(row_all, col_all)


def on_device(activations, out_grads, lengths, proj_in, proj_out):
    tokens = activations.shape[0] * L
    n_row = lax.axis_size("row")
    n_col = lax.axis_size("col")
    row_all, col_all = exchange(
        activations.reshape(tokens, -1),
        out_grads.reshape(tokens, -1),
        lengths, proj_in, proj_out, n_row, n_col,
    )
    block = row_all.shape[-1]
    return fisher(row_all.reshape(-1, block), col_all.reshape(CORES, -1, block))


def solution(mesh):
    placed = (
        P(("row", "col"), None, None),
        P(("row", "col"), None, None),
        P(("row", "col")),
        P(),
        P(),
    )
    return jax.shard_map(
        on_device, mesh=mesh, in_specs=placed, out_specs=P("row", "col"), check_vma=False
    )
```

```python
import functools
import math

import jax
import jax.numpy as jnp
from jax import lax
from jax.experimental import pallas as pl
from jax.experimental.pallas import tpu as pltpu
from jax.sharding import PartitionSpec as P

L = 64
CORES = 2
MESH = pl.DeviceIdType.MESH
MIB = 1024 * 1024


def exchange_kernel(
    n, lengths, act, og, w_in, w_out, row_ref, col_ref,
    act_v, og_v, w_in_v, w_out_v, in_acc, out_acc,
    in_f, out_f, in_peer, out_peer, wide, blocks,
    load_s, peer_s, peer_r, c1_s, c1_r, r1_s, r1_r, line_s, line_r, c2_s, c2_r, fw_s, fw_r, own_s,
):
    r, c = lax.axis_index("row"), lax.axis_index("col")
    k, m = r // CORES, r % CORES
    peer = (k * CORES + 1 - m, c)
    width = in_f.shape[1]
    local_ex = in_f.shape[0] // L
    pair_ex = CORES * local_ex
    per_block = blocks.shape[2] // width

    def loads(x, w, x_v, w_v, first):
        depth = x_v.shape[2]
        return [
            (
                pltpu.make_async_copy(x.at[:, pl.ds(q * depth, depth)], x_v.at[q], load_s.at[first + q, 0]),
                pltpu.make_async_copy(w.at[pl.ds(q * depth, depth)], w_v.at[q], load_s.at[first + q, 1]),
            )
            for q in range(x_v.shape[0])
        ]

    act_loads = loads(act, w_in, act_v, w_in_v, 0)
    og_loads = loads(og, w_out, og_v, w_out_v, len(act_loads))
    for pair in act_loads + og_loads:
        for copy in pair:
            copy.start()

    def project(pairs, x_v, w_v, acc):
        for q, pair in enumerate(pairs):
            for copy in pair:
                copy.wait()
            part = jnp.dot(x_v[q], w_v[q], preferred_element_type=jnp.float32)
            acc[...] = part if q == 0 else acc[...] + part

    def turn(start, d):
        return lax.rem(start + d + n, n)

    def send(src, dst, s, t, who):
        copy = pltpu.make_async_remote_copy(
            src_ref=src, dst_ref=dst, send_sem=s, recv_sem=t, device_id=who, device_id_type=MESH
        )
        copy.start()
        return copy

    barrier = pltpu.get_barrier_semaphore()
    pl.semaphore_signal(barrier, inc=1, device_id=peer, device_id_type=MESH)
    for d in range(1, n):
        pl.semaphore_signal(barrier, inc=1, device_id=(turn(k, d) * CORES + m, c), device_id_type=MESH)
        pl.semaphore_signal(barrier, inc=1, device_id=(r, turn(c, d)), device_id_type=MESH)

    project(act_loads, act_v, w_in_v, in_acc)
    in_f[...] = in_acc[...].astype(in_f.dtype)
    pl.semaphore_wait(barrier, 2 * n - 1)
    swaps = [send(in_f, in_peer, peer_s.at[0], peer_r.at[0], peer)]

    project(og_loads, og_v, w_out_v, out_acc)
    place = lax.broadcasted_iota(jnp.int32, (L, width), 0)
    for e in range(local_ex):
        rows = pl.ds(e * L, L)
        out_f[rows, :] = jnp.where(place < lengths[e], out_acc[rows, :], 0.0).astype(out_f.dtype)
    swaps.append(send(out_f, out_peer, peer_s.at[1], peer_r.at[1], peer))

    def outer(ins, outs, core):
        for e in range(local_ex):
            rows = pl.ds(e * L, L)
            grad = lax.dot_general(
                outs[rows, :], ins[rows, :], (((0,), (0,)), ((), ())), preferred_element_type=jnp.float32
            )
            start = pl.multiple_of((core * local_ex + e) * width, width)
            wide[pl.ds(start, width), :] = grad * (1.0 / jnp.sqrt(jnp.float32(L)))

    outer(in_f, out_f, m)
    for copy in swaps:
        copy.wait()
    outer(in_peer, out_peer, 1 - m)

    def form(q):
        for i in range(per_block):
            first = (q * CORES + m) * per_block + i
            blocks[q, :, i * width : (i + 1) * width] = wide[
                pl.ds(first, pair_ex, stride=width), :
            ].astype(blocks.dtype)

    to_col, to_row = [], []
    for d in range(1, n):
        q = turn(c, d)
        form(q)
        to_col.append(send(blocks.at[q], col_ref.at[m, c, k], c1_s.at[d], c1_r.at[d], (r, q)))
    form(c)
    for d in range(1, n):
        q = turn(k, d)
        to_row.append(send(blocks.at[q], row_ref.at[c, k], r1_s.at[d], r1_r.at[d], (q * CORES + m, c)))
    own = [
        pltpu.make_async_copy(blocks.at[k], row_ref.at[c, k], own_s.at[0]),
        pltpu.make_async_copy(blocks.at[c], col_ref.at[m, c, k], own_s.at[1]),
    ]
    for copy in own:
        copy.start()

    def broadcast(e, src):
        return [
            send(src, col_ref.at[m, turn(c, -e), k], c2_s.at[d, e], c2_r.at[d, e], (turn(k, d) * CORES + m, c))
            for d in range(1, n)
        ]

    across = [broadcast(0, blocks.at[c])]

    half = n // 2

    def hop(way, t, p):
        shard = row_ref.at[c - way * t, pl.ds(p * half, half)]
        w = (way + 1) // 2
        return pltpu.make_async_remote_copy(
            src_ref=shard,
            dst_ref=shard,
            send_sem=line_s.at[w, t, p],
            recv_sem=line_r.at[w, t, p],
            device_id=(r, c + way),
            device_id_type=MESH,
        )

    def arrival(way, t, p):
        shard = row_ref.at[c - way * t, pl.ds(p * half, half)]
        w = (way + 1) // 2
        return pltpu.make_async_remote_copy(
            src_ref=shard,
            dst_ref=shard,
            send_sem=line_s.at[w, t - 1, p],
            recv_sem=line_r.at[w, t - 1, p],
            device_id=(r, c - way),
            device_id_type=MESH,
        )

    def comes(way, t):
        return c - t >= 0 if way > 0 else c + t <= n - 1

    def goes(way):
        return c <= n - 2 if way > 0 else c >= 1

    def relay(t):
        for p in range(2):
            for way in (1, -1):
                if t > 0:

                    @pl.when(comes(way, t))
                    def _(way=way, p=p):
                        arrival(way, t, p).wait_recv()

                if t < n - 1:

                    @pl.when(jnp.logical_and(comes(way, t), goes(way)))
                    def _(way=way, p=p):
                        hop(way, t, p).start()

    for copy in to_row:
        copy.wait()
    own[0].wait()
    relay(0)

    for e in range(1, n):
        to_col[e - 1].wait_recv()
        across.append(broadcast(e, col_ref.at[m, turn(c, -e), k]))
    own[1].wait()
    mine = col_ref.at[m, :, k]
    passed = [send(mine, mine, fw_s.at[0], fw_r.at[0], peer)]
    for t in range(1, n - 1):
        relay(t)
    for d in range(1, n):
        for e in range(n):
            across[e][d - 1].wait_recv()
        piece = col_ref.at[m, :, turn(k, -d)]
        passed.append(send(piece, piece, fw_s.at[d], fw_r.at[d], peer))
    relay(n - 1)
    for copy in to_col + sum(across, []):
        copy.wait_send()
    for t in range(n - 1):
        for way in (1, -1):

            @pl.when(jnp.logical_and(comes(way, t), goes(way)))
            def _(way=way, t=t):
                for p in range(2):
                    hop(way, t, p).wait_send()

    for copy in passed:
        copy.wait()


def exchange(activations, out_grads, lengths, proj_in, proj_out, n_row, n_col):
    n = n_col
    assert n_row == CORES * n
    tokens, width = activations.shape[0], proj_in.shape[1]
    pair_ex = CORES * (tokens // L)
    block = width * width // n_row
    depth = math.gcd(proj_in.shape[0], proj_out.shape[0])
    ins, outs = proj_in.shape[0] // depth, proj_out.shape[0] // depth
    dma = pltpu.SemaphoreType.DMA
    return pl.pallas_call(
        functools.partial(exchange_kernel, n),
        in_specs=[pl.BlockSpec(memory_space=pltpu.SMEM)] + [pl.BlockSpec(memory_space=pl.ANY)] * 4,
        out_specs=[pl.BlockSpec(memory_space=pl.ANY)] * 2,
        out_shape=[
            jax.ShapeDtypeStruct((n, n, pair_ex, block), jnp.bfloat16),
            jax.ShapeDtypeStruct((CORES, n, n, pair_ex, block), jnp.bfloat16),
        ],
        scratch_shapes=[
            pltpu.VMEM((ins, tokens, depth), jnp.bfloat16),
            pltpu.VMEM((outs, tokens, depth), jnp.bfloat16),
            pltpu.VMEM((ins, depth, width), jnp.bfloat16),
            pltpu.VMEM((outs, depth, width), jnp.bfloat16),
        ]
        + [pltpu.VMEM((tokens, width), jnp.float32)] * 2
        + [pltpu.VMEM((tokens, width), jnp.bfloat16)] * 4
        + [
            pltpu.VMEM((pair_ex * width, width), jnp.float32),
            pltpu.VMEM((n, pair_ex, block), jnp.bfloat16),
            dma((ins + outs, 2)),
            dma((2,)), dma((2,)),
        ]
        + [dma((n,))] * 4
        + [dma((2, n - 1, 2))] * 2
        + [dma((n, n))] * 2
        + [dma((n,))] * 2
        + [dma((2,))],
        compiler_params=pltpu.CompilerParams(
            collective_id=0, has_side_effects=True, vmem_limit_bytes=58 * MIB
        ),
    )(lengths, activations, out_grads, proj_in, proj_out)


def fisher_kernel(scale, slots, parts, left_h, right_h, out, left, right, held, sems, load_s):
    h, i = pl.program_id(0), pl.program_id(1)
    tiles = pl.num_programs(1)
    steps = pl.num_programs(0) * tiles
    step = h * tiles + i
    _, tile, block = held.shape
    piece = tile // parts

    def writes(s):
        slot = lax.rem(s, slots)
        top, side = lax.rem(s, tiles) * tile, lax.div(s, tiles) * block
        return [
            pltpu.make_async_copy(
                held.at[slot, pl.ds(p * piece, piece)],
                out.at[pl.ds(top + p * piece, piece), pl.ds(pl.multiple_of(side, block), block)],
                sems.at[slot, p],
            )
            for p in range(parts)
        ]

    early = 2 * tile
    rest = left.shape[1] - early
    first = [
        pltpu.make_async_copy(right_h.at[0], right.at[0], load_s.at[0]),
        pltpu.make_async_copy(left_h.at[:, pl.ds(0, early)], left.at[:, pl.ds(0, early)], load_s.at[1]),
    ]
    later = [
        pltpu.make_async_copy(
            left_h.at[:, pl.ds(early, rest)], left.at[:, pl.ds(early, rest)], load_s.at[2]
        ),
        pltpu.make_async_copy(right_h.at[1], right.at[1], load_s.at[3]),
    ]

    @pl.when(step == 0)
    def _():
        for copy in first:
            copy.start()
        for copy in first:
            copy.wait()
        for copy in later:
            copy.start()

    @pl.when(step == 2)
    def _():
        later[0].wait()

    @pl.when(step == tiles)
    def _():
        later[1].wait()

    @pl.when(step >= slots)
    def _():
        for copy in writes(step - slots):
            copy.wait()

    slot = lax.rem(step, slots)
    held[slot] = scale * lax.dot_general(
        left[:, pl.ds(pl.multiple_of(i * tile, tile), tile)], right[h], (((0,), (0,)), ((), ())), preferred_element_type=jnp.float32
    )
    for copy in writes(step):
        copy.start()

    @pl.when(step == steps - 1)
    def _():
        for back in range(slots - 1, -1, -1):
            for copy in writes(step - back):
                copy.wait()


def fisher(row_all, col_all):
    total, rows = row_all.shape
    halves, _, block = col_all.shape
    tile, slots, parts = min(256, rows // 4), 4, 2
    return pl.pallas_call(
        functools.partial(fisher_kernel, 1.0 / total**0.5, slots, parts),
        grid=(halves, rows // tile),
        in_specs=[
            pl.BlockSpec(memory_space=pl.ANY),
            pl.BlockSpec(memory_space=pl.ANY),
        ],
        out_specs=pl.BlockSpec(memory_space=pl.ANY),
        out_shape=jax.ShapeDtypeStruct((rows, halves * block), jnp.float32),
        scratch_shapes=[
            pltpu.VMEM(row_all.shape, row_all.dtype),
            pltpu.VMEM(col_all.shape, col_all.dtype),
            pltpu.VMEM((slots, tile, block), jnp.float32),
            pltpu.SemaphoreType.DMA((slots, parts)),
            pltpu.SemaphoreType.DMA((4,)),
        ],
        compiler_params=pltpu.CompilerParams(vmem_limit_bytes=60 * MIB),
    )(row_all, col_all)


def on_device(activations, out_grads, lengths, proj_in, proj_out):
    tokens = activations.shape[0] * L
    n_row = lax.axis_size("row")
    n_col = lax.axis_size("col")
    row_all, col_all = exchange(
        activations.reshape(tokens, -1),
        out_grads.reshape(tokens, -1),
        lengths, proj_in, proj_out, n_row, n_col,
    )
    block = row_all.shape[-1]
    return fisher(row_all.reshape(-1, block), col_all.reshape(CORES, -1, block))


def solution(mesh):
    placed = (
        P(("row", "col"), None, None),
        P(("row", "col"), None, None),
        P(("row", "col")),
        P(),
        P(),
    )
    return jax.shard_map(
        on_device, mesh=mesh, in_specs=placed, out_specs=P("row", "col"), check_vma=False
    )
```

```python
import functools
import math

import jax
import jax.numpy as jnp
from jax import lax
from jax.experimental import pallas as pl
from jax.experimental.pallas import tpu as pltpu
from jax.sharding import PartitionSpec as P

L = 64
CORES = 2
MESH = pl.DeviceIdType.MESH
MIB = 1024 * 1024


def exchange_kernel(
    n, lengths, act, og, w_in, w_out, row_ref, col_ref,
    act_v, og_v, w_in_v, w_out_v, in_acc, out_acc,
    ins, outs, flipped, spread, blocks,
    load_s, peer_s, peer_r, c1_s, c1_r, r1_s, r1_r, line_s, line_r, c2_s, c2_r, fw_s, fw_r, own_s,
):
    r, c = lax.axis_index("row"), lax.axis_index("col")
    k, m = r // CORES, r % CORES
    peer = (k * CORES + 1 - m, c)
    width = ins.shape[1]
    tokens = act.shape[0]
    local_ex = tokens // L
    pair_ex = CORES * local_ex
    per_block = blocks.shape[2] // width

    def loads(x, w, x_v, w_v, first):
        depth = x_v.shape[2]
        return [
            (
                pltpu.make_async_copy(x.at[:, pl.ds(q * depth, depth)], x_v.at[q], load_s.at[first + q, 0]),
                pltpu.make_async_copy(w.at[pl.ds(q * depth, depth)], w_v.at[q], load_s.at[first + q, 1]),
            )
            for q in range(x_v.shape[0])
        ]

    act_loads = loads(act, w_in, act_v, w_in_v, 0)
    og_loads = loads(og, w_out, og_v, w_out_v, len(act_loads))
    for pair in act_loads + og_loads:
        for copy in pair:
            copy.start()

    def project(pairs, x_v, w_v, acc):
        for q, pair in enumerate(pairs):
            for copy in pair:
                copy.wait()
            part = jnp.dot(x_v[q], w_v[q], preferred_element_type=jnp.float32)
            acc[...] = part if q == 0 else acc[...] + part

    def turn(start, d):
        return lax.rem(start + d + n, n)

    def send(src, dst, s, t, who):
        copy = pltpu.make_async_remote_copy(
            src_ref=src, dst_ref=dst, send_sem=s, recv_sem=t, device_id=who, device_id_type=MESH
        )
        copy.start()
        return copy

    barrier = pltpu.get_barrier_semaphore()
    pl.semaphore_signal(barrier, inc=1, device_id=peer, device_id_type=MESH)
    for d in range(1, n):
        pl.semaphore_signal(barrier, inc=1, device_id=(turn(k, d) * CORES + m, c), device_id_type=MESH)
        pl.semaphore_signal(barrier, inc=1, device_id=(r, turn(c, d)), device_id_type=MESH)

    project(act_loads, act_v, w_in_v, in_acc)
    own_rows = pl.ds(pl.multiple_of(m * tokens, tokens), tokens)
    ins[own_rows, :] = in_acc[...].astype(ins.dtype)
    pl.semaphore_wait(barrier, 2 * n - 1)
    swaps = [send(ins.at[own_rows], ins.at[own_rows], peer_s.at[0], peer_r.at[0], peer)]

    project(og_loads, og_v, w_out_v, out_acc)
    place = lax.broadcasted_iota(jnp.int32, (L, width), 0)
    for e in range(local_ex):
        rows = pl.ds(e * L, L)
        out_acc[rows, :] = jnp.where(place < lengths[e], out_acc[rows, :], 0.0)
    outs[own_rows, :] = out_acc[...].astype(outs.dtype)
    swaps.append(send(outs.at[own_rows], outs.at[own_rows], peer_s.at[1], peer_r.at[1], peer))

    def flip(core):
        span = pl.ds(pl.multiple_of(core * tokens, tokens), tokens)
        flipped[:, span] = outs[span, :].astype(jnp.float32).T

    flip(m)
    for copy in swaps:
        copy.wait()
    flip(1 - m)

    whose = lax.broadcasted_iota(jnp.int32, (pair_ex, CORES * tokens), 1) // L
    mine_only = whose == lax.broadcasted_iota(jnp.int32, (pair_ex, CORES * tokens), 0)

    def form(q):
        first = pl.multiple_of((q * CORES + m) * per_block, per_block)
        group = flipped[pl.ds(first, per_block), :]
        for i in range(per_block):
            line = jnp.broadcast_to(group[i : i + 1, :], mine_only.shape)
            spread[pl.ds(i * pair_ex, pair_ex), :] = jnp.where(mine_only, line, 0.0).astype(spread.dtype)
        grad = jnp.dot(spread[...], ins[...], preferred_element_type=jnp.float32)
        grad = grad * (1.0 / jnp.sqrt(jnp.float32(L)))
        for i in range(per_block):
            blocks[q, :, i * width : (i + 1) * width] = grad[i * pair_ex : (i + 1) * pair_ex, :].astype(
                blocks.dtype
            )

    to_col, to_row = [], []
    for d in range(1, n):
        q = turn(c, d)
        form(q)
        to_col.append(send(blocks.at[q], col_ref.at[m, c, k], c1_s.at[d], c1_r.at[d], (r, q)))
    form(c)
    for d in range(1, n):
        q = turn(k, d)
        to_row.append(send(blocks.at[q], row_ref.at[c, k], r1_s.at[d], r1_r.at[d], (q * CORES + m, c)))
    own = [
        pltpu.make_async_copy(blocks.at[k], row_ref.at[c, k], own_s.at[0]),
        pltpu.make_async_copy(blocks.at[c], col_ref.at[m, c, k], own_s.at[1]),
    ]
    for copy in own:
        copy.start()

    def broadcast(e, src):
        return [
            send(src, col_ref.at[m, turn(c, -e), k], c2_s.at[d, e], c2_r.at[d, e], (turn(k, d) * CORES + m, c))
            for d in range(1, n)
        ]

    across = [broadcast(0, blocks.at[c])]

    half = n // 2

    def hop(way, t, p):
        shard = row_ref.at[c - way * t, pl.ds(p * half, half)]
        w = (way + 1) // 2
        return pltpu.make_async_remote_copy(
            src_ref=shard,
            dst_ref=shard,
            send_sem=line_s.at[w, t, p],
            recv_sem=line_r.at[w, t, p],
            device_id=(r, c + way),
            device_id_type=MESH,
        )

    def arrival(way, t, p):
        shard = row_ref.at[c - way * t, pl.ds(p * half, half)]
        w = (way + 1) // 2
        return pltpu.make_async_remote_copy(
            src_ref=shard,
            dst_ref=shard,
            send_sem=line_s.at[w, t - 1, p],
            recv_sem=line_r.at[w, t - 1, p],
            device_id=(r, c - way),
            device_id_type=MESH,
        )

    def comes(way, t):
        return c - t >= 0 if way > 0 else c + t <= n - 1

    def goes(way):
        return c <= n - 2 if way > 0 else c >= 1

    def relay(t):
        for p in range(2):
            for way in (1, -1):
                if t > 0:

                    @pl.when(comes(way, t))
                    def _(way=way, p=p):
                        arrival(way, t, p).wait_recv()

                if t < n - 1:

                    @pl.when(jnp.logical_and(comes(way, t), goes(way)))
                    def _(way=way, p=p):
                        hop(way, t, p).start()

    for copy in to_row:
        copy.wait()
    own[0].wait()
    relay(0)

    for e in range(1, n):
        to_col[e - 1].wait_recv()
        across.append(broadcast(e, col_ref.at[m, turn(c, -e), k]))
    own[1].wait()
    mine = col_ref.at[m, :, k]
    passed = [send(mine, mine, fw_s.at[0], fw_r.at[0], peer)]
    for t in range(1, n - 1):
        relay(t)
    for d in range(1, n):
        for e in range(n):
            across[e][d - 1].wait_recv()
        piece = col_ref.at[m, :, turn(k, -d)]
        passed.append(send(piece, piece, fw_s.at[d], fw_r.at[d], peer))
    relay(n - 1)
    for copy in to_col + sum(across, []):
        copy.wait_send()
    for t in range(n - 1):
        for way in (1, -1):

            @pl.when(jnp.logical_and(comes(way, t), goes(way)))
            def _(way=way, t=t):
                for p in range(2):
                    hop(way, t, p).wait_send()

    for copy in passed:
        copy.wait()


def exchange(activations, out_grads, lengths, proj_in, proj_out, n_row, n_col):
    n = n_col
    assert n_row == CORES * n
    tokens, width = activations.shape[0], proj_in.shape[1]
    pair_ex = CORES * (tokens // L)
    block = width * width // n_row
    depth = math.gcd(proj_in.shape[0], proj_out.shape[0])
    ins, outs = proj_in.shape[0] // depth, proj_out.shape[0] // depth
    dma = pltpu.SemaphoreType.DMA
    return pl.pallas_call(
        functools.partial(exchange_kernel, n),
        in_specs=[pl.BlockSpec(memory_space=pltpu.SMEM)] + [pl.BlockSpec(memory_space=pl.ANY)] * 4,
        out_specs=[pl.BlockSpec(memory_space=pl.ANY)] * 2,
        out_shape=[
            jax.ShapeDtypeStruct((n, n, pair_ex, block), jnp.bfloat16),
            jax.ShapeDtypeStruct((CORES, n, n, pair_ex, block), jnp.bfloat16),
        ],
        scratch_shapes=[
            pltpu.VMEM((ins, tokens, depth), jnp.bfloat16),
            pltpu.VMEM((outs, tokens, depth), jnp.bfloat16),
            pltpu.VMEM((ins, depth, width), jnp.bfloat16),
            pltpu.VMEM((outs, depth, width), jnp.bfloat16),
        ]
        + [pltpu.VMEM((tokens, width), jnp.float32)] * 2
        + [pltpu.VMEM((CORES * tokens, width), jnp.bfloat16)] * 2
        + [
            pltpu.VMEM((width, CORES * tokens), jnp.float32),
            pltpu.VMEM((width // n_row * pair_ex, CORES * tokens), jnp.bfloat16),
            pltpu.VMEM((n, pair_ex, block), jnp.bfloat16),
            dma((ins + outs, 2)),
            dma((2,)), dma((2,)),
        ]
        + [dma((n,))] * 4
        + [dma((2, n - 1, 2))] * 2
        + [dma((n, n))] * 2
        + [dma((n,))] * 2
        + [dma((2,))],
        compiler_params=pltpu.CompilerParams(
            collective_id=0, has_side_effects=True, vmem_limit_bytes=58 * MIB
        ),
    )(lengths, activations, out_grads, proj_in, proj_out)


def fisher_kernel(scale, slots, parts, left_h, right_h, out, left, right, held, sems, load_s):
    h, i = pl.program_id(0), pl.program_id(1)
    tiles = pl.num_programs(1)
    steps = pl.num_programs(0) * tiles
    step = h * tiles + i
    _, tile, block = held.shape
    piece = tile // parts

    def writes(s):
        slot = lax.rem(s, slots)
        top, side = lax.rem(s, tiles) * tile, lax.div(s, tiles) * block
        return [
            pltpu.make_async_copy(
                held.at[slot, pl.ds(p * piece, piece)],
                out.at[pl.ds(top + p * piece, piece), pl.ds(pl.multiple_of(side, block), block)],
                sems.at[slot, p],
            )
            for p in range(parts)
        ]

    early = 2 * tile
    rest = left.shape[1] - early
    first = [
        pltpu.make_async_copy(right_h.at[0], right.at[0], load_s.at[0]),
        pltpu.make_async_copy(left_h.at[:, pl.ds(0, early)], left.at[:, pl.ds(0, early)], load_s.at[1]),
    ]
    later = [
        pltpu.make_async_copy(
            left_h.at[:, pl.ds(early, rest)], left.at[:, pl.ds(early, rest)], load_s.at[2]
        ),
        pltpu.make_async_copy(right_h.at[1], right.at[1], load_s.at[3]),
    ]

    @pl.when(step == 0)
    def _():
        for copy in first:
            copy.start()
        for copy in first:
            copy.wait()
        for copy in later:
            copy.start()

    @pl.when(step == 2)
    def _():
        later[0].wait()

    @pl.when(step == tiles)
    def _():
        later[1].wait()

    @pl.when(step >= slots)
    def _():
        for copy in writes(step - slots):
            copy.wait()

    slot = lax.rem(step, slots)
    held[slot] = scale * lax.dot_general(
        left[:, pl.ds(pl.multiple_of(i * tile, tile), tile)], right[h], (((0,), (0,)), ((), ())), preferred_element_type=jnp.float32
    )
    for copy in writes(step):
        copy.start()

    @pl.when(step == steps - 1)
    def _():
        for back in range(slots - 1, -1, -1):
            for copy in writes(step - back):
                copy.wait()


def fisher(row_all, col_all):
    total, rows = row_all.shape
    halves, _, block = col_all.shape
    tile, slots, parts = min(256, rows // 4), 4, 2
    return pl.pallas_call(
        functools.partial(fisher_kernel, 1.0 / total**0.5, slots, parts),
        grid=(halves, rows // tile),
        in_specs=[
            pl.BlockSpec(memory_space=pl.ANY),
            pl.BlockSpec(memory_space=pl.ANY),
        ],
        out_specs=pl.BlockSpec(memory_space=pl.ANY),
        out_shape=jax.ShapeDtypeStruct((rows, halves * block), jnp.float32),
        scratch_shapes=[
            pltpu.VMEM(row_all.shape, row_all.dtype),
            pltpu.VMEM(col_all.shape, col_all.dtype),
            pltpu.VMEM((slots, tile, block), jnp.float32),
            pltpu.SemaphoreType.DMA((slots, parts)),
            pltpu.SemaphoreType.DMA((4,)),
        ],
        compiler_params=pltpu.CompilerParams(vmem_limit_bytes=60 * MIB),
    )(row_all, col_all)


def on_device(activations, out_grads, lengths, proj_in, proj_out):
    tokens = activations.shape[0] * L
    n_row = lax.axis_size("row")
    n_col = lax.axis_size("col")
    row_all, col_all = exchange(
        activations.reshape(tokens, -1),
        out_grads.reshape(tokens, -1),
        lengths, proj_in, proj_out, n_row, n_col,
    )
    block = row_all.shape[-1]
    return fisher(row_all.reshape(-1, block), col_all.reshape(CORES, -1, block))


def solution(mesh):
    placed = (
        P(("row", "col"), None, None),
        P(("row", "col"), None, None),
        P(("row", "col")),
        P(),
        P(),
    )
    return jax.shard_map(
        on_device, mesh=mesh, in_specs=placed, out_specs=P("row", "col"), check_vma=False
    )
```
